32 devices in a mesh: groups: 2 (over y), mp: 8 (over z, x), dp: 2 (over core).
Axes of the slice: x: 2, y: 2, z: 4, core: 2. Of those that a mesh axis runs over, the one named last changes fastest.
Arguments:
- inputs: bfloat16 [2048, 8192], P(('groups', 'dp'), 'mp'), parts along dimension 0, may hold values from -6 to 6
- rounding: bfloat16 [16384, 1024], P(('groups', 'dp'), 'mp'), parts along dimension 0, may hold values from -8 to 8
- codes: int32 [16384, 1024], P(('groups', 'dp'), 'mp'), parts along dimension 0, may hold values from 0 to 15
- scales: float32 [128, 8], P(('groups', 'dp'), 'mp'), parts along dimension 0, may hold values from 0.002 to 0.006
- pick: int32 [128, 8], P(('groups', 'dp'), 'mp'), parts along dimension 0, may hold values from 0 to 1
- target: bfloat16 [2048, 2048], P(('groups', 'dp'), 'mp'), parts along dimension 0, may hold values from -6 to 6
Outputs:
- grad: bfloat16 [16384, 1024], P(('groups', 'dp'), 'mp'), parts along dimension 0
The draws below stay inside these ranges and needn't reach their ends.
There are 2 independent parts, one for each index of `groups`. The reference program is written for one: setup_inputs(seed, part) draws one part's arguments, and reference() takes and returns one part's arrays. A program takes and returns all parts, laid end to end along the dimension named above; each array names one. Nothing has to cross between parts.
All inputs are finite; a program needn't handle non-finite values.
Results may differ from the reference program's by a relative error of at most 0.0085.
Values may be sent and summed in bfloat16 or wider, within the bound.
A program may use at most 64 MiB of HBM per device.

```python
import math
import jax
import jax.numpy as jnp
from jax import lax

D_IN = 8192
BLK = 128
TOK_DEV = 512
D_OUT = 2048
TOKENS = 1024
N_DP = 2


def plant(values, key, low, largest):
    extent = values.shape
    place = [jax.random.randint(jax.random.fold_in(key, axis), (), 0, extent[axis]) for axis in range(len(extent))]
    values = values.at[tuple(place)].set(low)
    longest = extent.index(max(extent))
    place[longest] = (place[longest] + 1) % extent[longest]
    return values.at[tuple(place)].set(largest)


def level_of(key, dims, shards, low, top_value):
    def one(dim, parts):
        heights = jax.random.uniform(jax.random.fold_in(jax.random.fold_in(key, 6), dim), (parts,), jnp.float32, low / len(shards), top_value / len(shards))
        return jnp.repeat(jnp.exp(heights), dims[dim] // parts).reshape((-1,) + (1,) * (len(dims) - dim - 1))

    gain = one(*shards[0])
    for cut in shards[1:]:
        gain = gain * one(*cut)
    return gain


def bell_draw(key, dims, deviation, limit, cuts=(), held_as=jnp.bfloat16):
    gain = level_of(key, dims, cuts, -0.22, 0.18) if cuts else 1.0
    entries = jax.random.normal(key, dims, jnp.float32) * deviation * gain
    return jnp.minimum(jnp.maximum(entries, -limit), limit).astype(held_as)


def setup_inputs(seed: int = 0, part: int = 0) -> dict:
    key_of = jax.random.split(jax.random.key(seed), 7)
    part_splits = jax.random.split(jax.random.fold_in(key_of[6], part), 7)
    inputs = bell_draw(part_splits[0], (TOKENS, D_IN), 1.0, 6.0, ((0, 2), (1, 8)))
    rounding = bell_draw(part_splits[1], (D_IN, D_OUT // 2), 2.0, 8.0, ((0, 2), (1, 8)))
    codes = plant(jax.random.randint(part_splits[2], (D_IN, D_OUT // 2), 0, 16), jax.random.fold_in(part_splits[2], 1), 0, 15).astype(jnp.int32)
    scales = jnp.clip(jnp.exp(math.log(0.006) - 1.09861225 * jax.random.uniform(part_splits[3], (D_IN // BLK, D_OUT // (2 * BLK)), jnp.float32) ** level_of(part_splits[3], (D_IN // BLK, D_OUT // (2 * BLK)), ((0, 2), (1, 8)), -0.2, 0.2)), 0.002, 0.006)
    pick = plant(jax.random.randint(part_splits[4], (D_IN // BLK, D_OUT // (2 * BLK)), 0, 2), jax.random.fold_in(part_splits[4], 1), 0, 1).astype(jnp.int32)
    target = bell_draw(part_splits[5], (TOKENS, D_OUT), 1.0, 6.0, ((0, 2), (1, 8)))
    return {"inputs": inputs, "rounding": rounding, "codes": codes, "scales": scales, "pick": pick, "target": target}


def expand_blocks(table, rows, cols):
    row_blocks, col_blocks = table.shape
    spread = jnp.broadcast_to(table[:, None, :, None], (row_blocks, BLK, col_blocks, BLK))
    return spread.reshape(rows, cols)

def soft_weights(rounding, codes, scales, pick):
    rows, half = rounding.shape
    nblocks = half // BLK
    levels = (codes - 8).astype(jnp.float32)
    soft = jax.nn.sigmoid(rounding.astype(jnp.float32))
    factor = expand_blocks(scales, rows, half)
    kept_weight = (factor * jnp.clip(levels + soft, -8.0, 7.0)).astype(jnp.bfloat16)
    chosen = expand_blocks(pick, rows, half).reshape(rows, nblocks, 1, BLK)
    places = jnp.arange(2, dtype=jnp.int32).reshape(1, 1, 2, 1)
    spread = jnp.broadcast_to(kept_weight.reshape(rows, nblocks, 1, BLK), (rows, nblocks, 2, BLK))
    weight = jnp.where(chosen == places, spread, jnp.zeros((), jnp.bfloat16)).reshape(rows, 2 * half)
    slope = soft * (1.0 - soft) * (levels < 6.5).astype(jnp.float32)
    return (weight, slope, chosen)

def compact(full, chosen):
    rows = full.shape[0]
    nblocks = chosen.shape[1]
    pieces = full.reshape(rows, nblocks, 2, BLK)
    return jnp.where(chosen[:, :, 0, :] == 0, pieces[:, :, 0, :], pieces[:, :, 1, :]).reshape(rows, nblocks * BLK)

def reference(inputs, rounding, codes, scales, pick, target):
    scale_root = math.sqrt(TOKENS)

    def column(index):
        start = index * BLK
        block_vars = lax.dynamic_slice_in_dim(rounding, start, BLK, 1)
        block_codes = lax.dynamic_slice_in_dim(codes, start, BLK, 1)
        block_scales = lax.dynamic_slice_in_dim(scales, index, 1, 1)
        block_pick = lax.dynamic_slice_in_dim(pick, index, 1, 1)
        block_target = lax.dynamic_slice_in_dim(target, 2 * start, 2 * BLK, 1)
        weight, slope, chosen = soft_weights(block_vars, block_codes, block_scales, block_pick)
        outputs = jnp.dot(inputs, weight, preferred_element_type=jnp.float32)
        resid = ((outputs - block_target.astype(jnp.float32)) / scale_root).astype(jnp.bfloat16)
        total = jnp.zeros((D_IN, 2 * BLK), jnp.float32)
        for part in range(N_DP):
            rows = inputs[part * TOK_DEV:(part + 1) * TOK_DEV]
            part_resid = resid[part * TOK_DEV:(part + 1) * TOK_DEV]
            term = lax.dot_general(rows, part_resid, (((0,), (0,)), ((), ())), preferred_element_type=jnp.float32)
            total = total + lax.optimization_barrier(term.astype(jnp.bfloat16)).astype(jnp.float32)
        return (compact(total, chosen) * slope).astype(jnp.bfloat16)
    blocks = lax.map(column, jnp.arange(D_OUT // (2 * BLK), dtype=jnp.int32))
    return jnp.transpose(blocks, (1, 0, 2)).reshape(D_IN, D_OUT // 2)
```

```python
import math

import jax
import jax.numpy as jnp
from jax import lax
from jax.experimental import pallas as pl
from jax.experimental.pallas import tpu as pltpu
from jax.sharding import PartitionSpec as P

BLK = 128
MESH = pl.DeviceIdType.MESH
NZ, NX = 4, 2


def expand_blocks(table, rows, cols):
    row_blocks, col_blocks = table.shape
    spread = jnp.broadcast_to(table[:, None, :, None], (row_blocks, BLK, col_blocks, BLK))
    return spread.reshape(rows, cols)


def soft_weights(rounding, codes, scales, pick):
    rows, half = rounding.shape
    nblocks = half // BLK
    levels = (codes - 8).astype(jnp.float32)
    soft = jax.nn.sigmoid(rounding.astype(jnp.float32))
    factor = expand_blocks(scales, rows, half)
    kept_weight = (factor * jnp.clip(levels + soft, -8.0, 7.0)).astype(jnp.bfloat16)
    chosen = expand_blocks(pick, rows, half).reshape(rows, nblocks, 1, BLK)
    places = jnp.arange(2, dtype=jnp.int32).reshape(1, 1, 2, 1)
    spread = jnp.broadcast_to(kept_weight.reshape(rows, nblocks, 1, BLK), (rows, nblocks, 2, BLK))
    weight = jnp.where(chosen == places, spread, jnp.zeros((), jnp.bfloat16)).reshape(
        rows, 2 * half
    )
    slope = soft * (1.0 - soft) * (levels < 6.5).astype(jnp.float32)
    return (weight, slope, chosen)


def compact(full, chosen):
    rows = full.shape[0]
    nblocks = chosen.shape[1]
    pieces = full.reshape(rows, nblocks, 2, BLK)
    return jnp.where(chosen[:, :, 0, :] == 0, pieces[:, :, 0, :], pieces[:, :, 1, :]).reshape(
        rows, nblocks * BLK
    )


def body(inputs, rounding, codes, scales, pick, target):
    weight, slope, chosen = soft_weights(rounding, codes, scales, pick)
    tok_rows = inputs.shape[0]
    scale_root = math.sqrt(tok_rows * lax.axis_size("dp"))
    gathered = lax.all_gather(inputs, "mp", axis=1, tiled=True)
    columns = gathered
    outputs = jnp.dot(
        columns,
        lax.all_gather(weight, "dp", axis=0, tiled=True),
        preferred_element_type=jnp.float32,
    )
    resid = ((outputs - target.astype(jnp.float32)) / scale_root).astype(jnp.bfloat16)
    columns = gathered
    weight_grad = lax.psum_scatter(
        lax.dot_general(
            columns, resid, (((0,), (0,)), ((), ())), preferred_element_type=jnp.float32
        ).astype(jnp.bfloat16),
        "dp",
        scatter_dimension=0,
        tiled=True,
    ).astype(jnp.float32)
    return (compact(weight_grad, chosen) * slope).astype(jnp.bfloat16)


def order(step, z):
    far = z // 2
    near = z * (1 - far) + (NZ - 1 - z) * far
    late = step // 2
    place = (1 - late) * ((step + near) % 2) + late * step
    return (1 - far) * place + far * (NZ - 1 - place)


def kernel(
    inputs, rounding, codes, scales, pick, target, out,
    gathered, turned, weight, slope, rounding_v, codes_v, outputs, resid,
    pick_own, pick_other, scale_rows, outgoing, incoming, kept,
    local_sem, recv_sem, x_sem, up_sem, down_sem, w_send, w_recv, p_send, p_recv, g_send, g_recv,
):
    tokens, features = inputs.shape
    rows = rounding.shape[0]
    shards_each = rows // features
    blocks = features // BLK
    me = lax.axis_index("mp")
    dp = lax.axis_index("dp")
    z, x = me // NX, me % NX
    other = 1 - dp
    beside = {"mp": z * NX + (1 - x)}
    above = {"mp": me + NX}
    below = {"mp": me - NX}
    twin = {"dp": other}

    def remote(source, dest, send, recv, device):
        return pltpu.make_async_remote_copy(
            src_ref=source, dst_ref=dest, send_sem=send, recv_sem=recv,
            device_id=device, device_id_type=MESH,
        )

    own = pltpu.make_async_copy(inputs, gathered.at[me], local_sem.at[0])
    get_rounding = pltpu.make_async_copy(rounding, rounding_v, local_sem.at[1])
    get_codes = pltpu.make_async_copy(codes, codes_v, local_sem.at[2])
    own.start()
    get_rounding.start()
    get_codes.start()

    barrier = pltpu.get_barrier_semaphore()
    pl.semaphore_signal(barrier, inc=1, device_id=beside, device_id_type=MESH)
    pl.semaphore_signal(barrier, inc=1, device_id=twin, device_id_type=MESH)

    @pl.when(z < NZ - 1)
    def _():
        pl.semaphore_signal(barrier, inc=1, device_id=above, device_id_type=MESH)

    @pl.when(z > 0)
    def _():
        pl.semaphore_signal(barrier, inc=1, device_id=below, device_id_type=MESH)

    pl.semaphore_wait(barrier, 2 + (z + NZ - 2) // (NZ - 1) + (2 * NZ - 3 - z) // (NZ - 1))

    def sends(step):
        column = order(step, z)
        slot = column * NX + x
        block = gathered.at[slot]
        arrive = recv_sem.at[slot]
        return (
            (column <= z, z < NZ - 1, remote(block, block, up_sem.at[step], arrive, above)),
            (column >= z, z > 0, remote(block, block, down_sem.at[step], arrive, below)),
            (True, True, remote(block, block, x_sem.at[step], arrive, beside)),
        )

    def each_send(step, act):
        for first, second, copy in sends(step):
            if first is True:
                act(copy)
            else:
                @pl.when(jnp.logical_and(first, second))
                def _():
                    act(copy)

    def arrived(slot):
        block = gathered.at[slot]
        remote(block, block, x_sem.at[0], recv_sem.at[slot], beside).wait_recv()

    own.wait()
    each_send(0, lambda copy: copy.start())

    pick_own[...] = jnp.broadcast_to(pick[...].astype(jnp.float32), pick_own.shape)
    scale_rows[...] = jnp.broadcast_to(scales[...], scale_rows.shape)
    send_pick = remote(pick_own, pick_other, p_send, p_recv, twin)
    send_pick.start()
    get_rounding.wait()
    get_codes.wait()

    def soft_block(index, carry):
        at = pl.ds(pl.multiple_of(index * BLK, BLK), BLK)
        levels = (codes_v[at, :] - 8).astype(jnp.float32)
        soft = jax.nn.sigmoid(rounding_v[at, :].astype(jnp.float32))
        factor = scale_rows[pl.ds(index, 1), :]
        chosen = pick_own[pl.ds(index, 1), :]
        value = factor * jnp.clip(levels + soft, -8.0, 7.0)
        first = jnp.broadcast_to(chosen, value.shape) < 0.5
        here = pl.ds(pl.multiple_of(dp * rows + index * BLK, BLK), BLK)
        weight[here, :BLK] = jnp.where(first, value, 0.0).astype(jnp.bfloat16)
        weight[here, BLK:] = jnp.where(first, 0.0, value).astype(jnp.bfloat16)
        slope[at, :] = soft * (1.0 - soft) * (levels < 6.5).astype(jnp.float32)
        return carry

    lax.fori_loop(0, rows // BLK, soft_block, 0)
    mine = weight.at[pl.ds(pl.multiple_of(dp * rows, BLK), rows), :]
    send_weight = remote(mine, mine, w_send, w_recv, twin)
    send_weight.start()
    outputs[...] = jnp.zeros_like(outputs)
    send_weight.wait()
    send_pick.wait()

    width = 2 * BLK

    def add(slot):
        def part(index, carry):
            at = pl.ds(pl.multiple_of(index * width, width), width)
            here = pl.ds(pl.multiple_of(slot * features + index * width, width), width)
            piece = gathered[slot, :, at]
            outputs[...] += jnp.dot(piece, weight[here, :], preferred_element_type=jnp.float32)
            turned[here, :] = piece.T
            return carry

        lax.fori_loop(0, features // width, part, 0)

    add(me)

    def column_step(step, carry):
        slot = order(step, z) * NX + x
        arrived(slot)
        each_send(step, lambda copy: copy.start())
        add(slot)
        return carry

    lax.fori_loop(1, NZ, column_step, 0)

    def beside_step(step, carry):
        slot = order(step, z) * NX + (1 - x)
        arrived(slot)
        add(slot)
        return carry

    lax.fori_loop(0, NZ, beside_step, 0)

    scale_root = math.sqrt(tokens * 2)
    resid[...] = ((outputs[...] - target[...].astype(jnp.float32)) / scale_root).astype(jnp.bfloat16)

    def block_grad(start, index, table):
        here = pl.ds(pl.multiple_of(start + index * width, width), width)
        full = jnp.dot(turned[here, :], resid[...], preferred_element_type=jnp.float32)
        parts = []
        for half in range(2):
            chosen = table[pl.ds(2 * index + half, 1), :]
            piece = full[half * BLK:(half + 1) * BLK]
            first = jnp.broadcast_to(chosen, (BLK, BLK)) < 0.5
            parts.append(jnp.where(first, piece[:, :BLK], piece[:, BLK:]).astype(jnp.bfloat16))
        return parts

    steps = features // width

    def grad_send(shard):
        at = pl.ds(pl.multiple_of(shard * features, features), features)
        return remote(
            outgoing.at[at, :], incoming.at[at, :], g_send.at[shard], g_recv.at[shard], twin
        )

    def send_shard(shard, carry):
        def part(index, carry):
            index = shard * steps + index
            first, second = block_grad(other * rows, index, pick_other)
            outgoing[pl.ds(pl.multiple_of(index * width, width), BLK), :] = first
            outgoing[pl.ds(pl.multiple_of(index * width + BLK, BLK), BLK), :] = second
            return carry

        lax.fori_loop(0, steps, part, 0)
        grad_send(shard).start()
        return carry

    lax.fori_loop(0, shards_each, send_shard, 0)

    def keep_shard(index, carry):
        first, second = block_grad(dp * rows, index, pick_own)
        kept[pl.ds(pl.multiple_of(index * width, width), BLK), :] = first
        kept[pl.ds(pl.multiple_of(index * width + BLK, BLK), BLK), :] = second
        return carry

    lax.fori_loop(0, shards_each * steps, keep_shard, 0)

    def finish(shard, carry):
        grad_send(shard).wait()

        def part(index, carry):
            at = pl.ds(pl.multiple_of(shard * features + index * BLK, BLK), BLK)
            total = kept[at, :].astype(jnp.float32) + incoming[at, :].astype(jnp.float32)
            out[at, :] = (total * slope[at, :]).astype(jnp.bfloat16)
            return carry

        return lax.fori_loop(0, blocks, part, carry)

    lax.fori_loop(0, shards_each, finish, 0)

    def drain(step, carry):
        each_send(step, lambda copy: copy.wait_send())
        return carry

    lax.fori_loop(0, NZ, drain, 0)


def fused(inputs, rounding, codes, scales, pick, target):
    tokens, features = inputs.shape
    rows = rounding.shape[0]
    shards = NZ * NX
    every = shards * features
    anywhere = pl.BlockSpec(memory_space=pl.ANY)
    near = pl.BlockSpec(memory_space=pltpu.VMEM)
    bf16, f32 = jnp.bfloat16, jnp.float32
    dma = pltpu.SemaphoreType.DMA
    return pl.pallas_call(
        kernel,
        out_shape=jax.ShapeDtypeStruct((rows, BLK), bf16),
        in_specs=[anywhere, anywhere, anywhere, near, near, near],
        out_specs=near,
        scratch_shapes=[
            pltpu.VMEM((shards, tokens, features), bf16),
            pltpu.VMEM((every, tokens), bf16),
            pltpu.VMEM((every, 2 * BLK), bf16),
            pltpu.VMEM((rows, BLK), f32),
            pltpu.VMEM((rows, BLK), bf16),
            pltpu.VMEM((rows, BLK), jnp.int32),
            pltpu.VMEM((tokens, 2 * BLK), f32),
            pltpu.VMEM((tokens, 2 * BLK), bf16),
            pltpu.VMEM((rows // BLK, BLK), f32),
            pltpu.VMEM((rows // BLK, BLK), f32),
            pltpu.VMEM((rows // BLK, BLK), f32),
            pltpu.VMEM((rows, BLK), bf16),
            pltpu.VMEM((rows, BLK), bf16),
            pltpu.VMEM((rows, BLK), bf16),
            dma((3,)),
            dma((shards,)),
            dma((NZ,)),
            dma((NZ,)),
            dma((NZ,)),
            dma(()),
            dma(()),
            dma(()),
            dma(()),
            dma((rows // features,)),
            dma((rows // features,)),
        ],
        compiler_params=pltpu.CompilerParams(
            collective_id=0, has_side_effects=True, vmem_limit_bytes=50 * 1024 * 1024
        ),
    )(inputs, rounding, codes, scales, pick, target)


def solution(mesh):
    grid = mesh.shape["mp"] == NZ * NX and mesh.shape["dp"] == 2
    run = fused if grid else body
    in_specs = (
        P(("groups", "dp"), "mp"),
        P(("groups", "dp"), "mp"),
        P(("groups", "dp"), "mp"),
        P(("groups", "dp"), "mp"),
        P(("groups", "dp"), "mp"),
        P(("groups", "dp"), "mp"),
    )
    out_specs = P(("groups", "dp"), "mp")
    return jax.shard_map(run, mesh=mesh, in_specs=in_specs, out_specs=out_specs, check_vma=False)
```

```python
import math

import jax
import jax.numpy as jnp
from jax import lax
from jax.experimental import pallas as pl
from jax.experimental.pallas import tpu as pltpu
from jax.sharding import PartitionSpec as P

BLK = 128
MESH = pl.DeviceIdType.MESH
NZ, NX = 4, 2


def expand_blocks(table, rows, cols):
    row_blocks, col_blocks = table.shape
    spread = jnp.broadcast_to(table[:, None, :, None], (row_blocks, BLK, col_blocks, BLK))
    return spread.reshape(rows, cols)


def soft_weights(rounding, codes, scales, pick):
    rows, half = rounding.shape
    nblocks = half // BLK
    levels = (codes - 8).astype(jnp.float32)
    soft = jax.nn.sigmoid(rounding.astype(jnp.float32))
    factor = expand_blocks(scales, rows, half)
    kept_weight = (factor * jnp.clip(levels + soft, -8.0, 7.0)).astype(jnp.bfloat16)
    chosen = expand_blocks(pick, rows, half).reshape(rows, nblocks, 1, BLK)
    places = jnp.arange(2, dtype=jnp.int32).reshape(1, 1, 2, 1)
    spread = jnp.broadcast_to(kept_weight.reshape(rows, nblocks, 1, BLK), (rows, nblocks, 2, BLK))
    weight = jnp.where(chosen == places, spread, jnp.zeros((), jnp.bfloat16)).reshape(
        rows, 2 * half
    )
    slope = soft * (1.0 - soft) * (levels < 6.5).astype(jnp.float32)
    return (weight, slope, chosen)


def compact(full, chosen):
    rows = full.shape[0]
    nblocks = chosen.shape[1]
    pieces = full.reshape(rows, nblocks, 2, BLK)
    return jnp.where(chosen[:, :, 0, :] == 0, pieces[:, :, 0, :], pieces[:, :, 1, :]).reshape(
        rows, nblocks * BLK
    )


def body(inputs, rounding, codes, scales, pick, target):
    weight, slope, chosen = soft_weights(rounding, codes, scales, pick)
    tok_rows = inputs.shape[0]
    scale_root = math.sqrt(tok_rows * lax.axis_size("dp"))
    gathered = lax.all_gather(inputs, "mp", axis=1, tiled=True)
    columns = gathered
    outputs = jnp.dot(
        columns,
        lax.all_gather(weight, "dp", axis=0, tiled=True),
        preferred_element_type=jnp.float32,
    )
    resid = ((outputs - target.astype(jnp.float32)) / scale_root).astype(jnp.bfloat16)
    columns = gathered
    weight_grad = lax.psum_scatter(
        lax.dot_general(
            columns, resid, (((0,), (0,)), ((), ())), preferred_element_type=jnp.float32
        ).astype(jnp.bfloat16),
        "dp",
        scatter_dimension=0,
        tiled=True,
    ).astype(jnp.float32)
    return (compact(weight_grad, chosen) * slope).astype(jnp.bfloat16)


def order(step, z):
    far = z // 2
    near = z * (1 - far) + (NZ - 1 - z) * far
    late = step // 2
    place = (1 - late) * ((step + near) % 2) + late * step
    return (1 - far) * place + far * (NZ - 1 - place)


def kernel(
    inputs, rounding, codes, scales, pick, target, out,
    gathered, turned, weight, slope, rounding_v, codes_v, outputs, resid,
    pick_own, pick_other, scale_rows, outgoing, incoming, kept,
    local_sem, recv_sem, x_sem, up_sem, down_sem, w_send, w_recv, p_send, p_recv, g_send, g_recv,
):
    tokens, features = inputs.shape
    rows = rounding.shape[0]
    shards_each = rows // features
    blocks = features // BLK
    me = lax.axis_index("mp")
    dp = lax.axis_index("dp")
    z, x = me // NX, me % NX
    other = 1 - dp
    beside = {"mp": z * NX + (1 - x)}
    above = {"mp": me + NX}
    below = {"mp": me - NX}
    twin = {"dp": other}

    def remote(source, dest, send, recv, device):
        return pltpu.make_async_remote_copy(
            src_ref=source, dst_ref=dest, send_sem=send, recv_sem=recv,
            device_id=device, device_id_type=MESH,
        )

    own = pltpu.make_async_copy(inputs, gathered.at[me], local_sem.at[0])
    get_rounding = pltpu.make_async_copy(rounding, rounding_v, local_sem.at[1])
    get_codes = pltpu.make_async_copy(codes, codes_v, local_sem.at[2])
    own.start()
    get_rounding.start()
    get_codes.start()

    barrier = pltpu.get_barrier_semaphore()
    pl.semaphore_signal(barrier, inc=1, device_id=beside, device_id_type=MESH)
    pl.semaphore_signal(barrier, inc=1, device_id=twin, device_id_type=MESH)

    @pl.when(z < NZ - 1)
    def _():
        pl.semaphore_signal(barrier, inc=1, device_id=above, device_id_type=MESH)

    @pl.when(z > 0)
    def _():
        pl.semaphore_signal(barrier, inc=1, device_id=below, device_id_type=MESH)

    pl.semaphore_wait(barrier, 2 + (z + NZ - 2) // (NZ - 1) + (2 * NZ - 3 - z) // (NZ - 1))

    lead = tokens * 5 // 512 * 16
    middle = lead + (tokens - lead + 16) // 32 * 16
    bounds = ((lead, middle), (middle, tokens), (0, lead))

    def piece_copies(step, side, piece):
        column = order(step, z)
        slot = column * NX + (x if side == 0 else 1 - x)
        start, stop = bounds[piece]
        block = gathered.at[slot, pl.ds(start, stop - start), :]
        arrive = recv_sem.at[slot, piece]
        lane = piece + side
        return (
            (column <= z, z < NZ - 1, lambda: remote(block, block, up_sem.at[step, lane], arrive, above)),
            (column >= z, z > 0, lambda: remote(block, block, down_sem.at[step, lane], arrive, below)),
            lambda: remote(block, block, x_sem.at[step, piece], arrive, beside),
        )

    def along(step, side, piece, act):
        for first, second, copy in piece_copies(step, side, piece)[:2]:

            @pl.when(jnp.logical_and(first, second))
            def _():
                act(copy())

    def across(step, piece, act):
        act(piece_copies(step, 0, piece)[2]())

    def arrived(step, side, piece):
        piece_copies(step, side, piece)[2]().wait_recv()

    def begin(copy):
        copy.start()

    own.wait()
    across(0, 2, begin)
    for piece in range(3):
        along(0, 0, piece, begin)
        if piece < 2:
            across(0, piece, begin)

    pick_own[...] = jnp.broadcast_to(pick[...].astype(jnp.float32), pick_own.shape)
    scale_rows[...] = jnp.broadcast_to(scales[...], scale_rows.shape)
    send_pick = remote(pick_own, pick_other, p_send, p_recv, twin)
    send_pick.start()
    get_rounding.wait()
    get_codes.wait()

    def soft_block(index, carry):
        at = pl.ds(pl.multiple_of(index * BLK, BLK), BLK)
        levels = (codes_v[at, :] - 8).astype(jnp.float32)
        soft = jax.nn.sigmoid(rounding_v[at, :].astype(jnp.float32))
        factor = scale_rows[pl.ds(index, 1), :]
        chosen = pick_own[pl.ds(index, 1), :]
        value = factor * jnp.clip(levels + soft, -8.0, 7.0)
        first = jnp.broadcast_to(chosen, value.shape) < 0.5
        here = pl.ds(pl.multiple_of(dp * rows + index * BLK, BLK), BLK)
        weight[here, :BLK] = jnp.where(first, value, 0.0).astype(jnp.bfloat16)
        weight[here, BLK:] = jnp.where(first, 0.0, value).astype(jnp.bfloat16)
        slope[at, :] = soft * (1.0 - soft) * (levels < 6.5).astype(jnp.float32)
        return carry

    lax.fori_loop(0, rows // BLK, soft_block, 0)
    mine = weight.at[pl.ds(pl.multiple_of(dp * rows, BLK), rows), :]
    send_weight = remote(mine, mine, w_send, w_recv, twin)
    send_weight.start()
    arrived(0, 1, 2)
    along(0, 1, 2, begin)
    outputs[...] = jnp.zeros_like(outputs)
    send_weight.wait()
    send_pick.wait()

    width = 2 * BLK

    def add(slot):
        def part(index, carry):
            at = pl.ds(pl.multiple_of(index * width, width), width)
            here = pl.ds(pl.multiple_of(slot * features + index * width, width), width)
            piece = gathered[slot, :, at]
            outputs[...] += jnp.dot(piece, weight[here, :], preferred_element_type=jnp.float32)
            turned[here, :] = piece.T
            return carry

        lax.fori_loop(0, features // width, part, 0)

    add(me)

    def column_step(step, carry):
        for piece in range(2):
            arrived(step, 0, piece)
            along(step, 0, piece, begin)
            across(step, piece, begin)
        return carry

    lax.fori_loop(1, NZ, column_step, 0)
    for piece in range(2):
        arrived(0, 1, piece)
    add(z * NX + 1 - x)

    def lead_step(step, carry):
        for side in range(2):
            arrived(step, side, 2)
            along(step, side, 2, begin)
        column = order(step, z)
        add(column * NX + x)
        for piece in range(2):
            arrived(step, 1, piece)
        add(column * NX + 1 - x)
        return carry

    lax.fori_loop(1, NZ, lead_step, 0)

    scale_root = math.sqrt(tokens * 2)
    resid[...] = ((outputs[...] - target[...].astype(jnp.float32)) / scale_root).astype(jnp.bfloat16)

    def block_grad(start, index, table):
        here = pl.ds(pl.multiple_of(start + index * width, width), width)
        full = jnp.dot(turned[here, :], resid[...], preferred_element_type=jnp.float32)
        parts = []
        for half in range(2):
            chosen = table[pl.ds(2 * index + half, 1), :]
            piece = full[half * BLK:(half + 1) * BLK]
            first = jnp.broadcast_to(chosen, (BLK, BLK)) < 0.5
            parts.append(jnp.where(first, piece[:, :BLK], piece[:, BLK:]).astype(jnp.bfloat16))
        return parts

    steps = features // width

    def grad_send(shard):
        at = pl.ds(pl.multiple_of(shard * features, features), features)
        return remote(
            outgoing.at[at, :], incoming.at[at, :], g_send.at[shard], g_recv.at[shard], twin
        )

    def send_shard(shard, carry):
        def part(index, carry):
            index = shard * steps + index
            first, second = block_grad(other * rows, index, pick_other)
            outgoing[pl.ds(pl.multiple_of(index * width, width), BLK), :] = first
            outgoing[pl.ds(pl.multiple_of(index * width + BLK, BLK), BLK), :] = second
            return carry

        lax.fori_loop(0, steps, part, 0)
        grad_send(shard).start()
        return carry

    lax.fori_loop(0, shards_each, send_shard, 0)

    def keep_shard(index, carry):
        first, second = block_grad(dp * rows, index, pick_own)
        kept[pl.ds(pl.multiple_of(index * width, width), BLK), :] = first
        kept[pl.ds(pl.multiple_of(index * width + BLK, BLK), BLK), :] = second
        return carry

    lax.fori_loop(0, shards_each * steps, keep_shard, 0)

    def finish(shard, carry):
        grad_send(shard).wait()

        def part(index, carry):
            at = pl.ds(pl.multiple_of(shard * features + index * BLK, BLK), BLK)
            total = kept[at, :].astype(jnp.float32) + incoming[at, :].astype(jnp.float32)
            out[at, :] = (total * slope[at, :]).astype(jnp.bfloat16)
            return carry

        return lax.fori_loop(0, blocks, part, carry)

    lax.fori_loop(0, shards_each, finish, 0)

    def finished(copy):
        copy.wait_send()

    def drain(step, carry):
        for piece in range(3):
            along(step, 0, piece, finished)
        along(step, 1, 2, finished)
        for piece in range(2):
            across(step, piece, finished)
        return carry

    across(0, 2, finished)
    lax.fori_loop(0, NZ, drain, 0)


def fused(inputs, rounding, codes, scales, pick, target):
    tokens, features = inputs.shape
    rows = rounding.shape[0]
    shards = NZ * NX
    every = shards * features
    anywhere = pl.BlockSpec(memory_space=pl.ANY)
    near = pl.BlockSpec(memory_space=pltpu.VMEM)
    bf16, f32 = jnp.bfloat16, jnp.float32
    dma = pltpu.SemaphoreType.DMA
    return pl.pallas_call(
        kernel,
        out_shape=jax.ShapeDtypeStruct((rows, BLK), bf16),
        in_specs=[anywhere, anywhere, anywhere, near, near, near],
        out_specs=near,
        scratch_shapes=[
            pltpu.VMEM((shards, tokens, features), bf16),
            pltpu.VMEM((every, tokens), bf16),
            pltpu.VMEM((every, 2 * BLK), bf16),
            pltpu.VMEM((rows, BLK), f32),
            pltpu.VMEM((rows, BLK), bf16),
            pltpu.VMEM((rows, BLK), jnp.int32),
            pltpu.VMEM((tokens, 2 * BLK), f32),
            pltpu.VMEM((tokens, 2 * BLK), bf16),
            pltpu.VMEM((rows // BLK, BLK), f32),
            pltpu.VMEM((rows // BLK, BLK), f32),
            pltpu.VMEM((rows // BLK, BLK), f32),
            pltpu.VMEM((rows, BLK), bf16),
            pltpu.VMEM((rows, BLK), bf16),
            pltpu.VMEM((rows, BLK), bf16),
            dma((3,)),
            dma((shards, 3)),
            dma((NZ, 3)),
            dma((NZ, 4)),
            dma((NZ, 4)),
            dma(()),
            dma(()),
            dma(()),
            dma(()),
            dma((rows // features,)),
            dma((rows // features,)),
        ],
        compiler_params=pltpu.CompilerParams(
            collective_id=0, has_side_effects=True, vmem_limit_bytes=60 * 1024 * 1024
        ),
    )(inputs, rounding, codes, scales, pick, target)


def solution(mesh):
    grid = mesh.shape["mp"] == NZ * NX and mesh.shape["dp"] == 2
    run = fused if grid else body
    in_specs = (
        P(("groups", "dp"), "mp"),
        P(("groups", "dp"), "mp"),
        P(("groups", "dp"), "mp"),
        P(("groups", "dp"), "mp"),
        P(("groups", "dp"), "mp"),
        P(("groups", "dp"), "mp"),
    )
    out_specs = P(("groups", "dp"), "mp")
    return jax.shard_map(run, mesh=mesh, in_specs=in_specs, out_specs=out_specs, check_vma=False)
```

```python
import math

import jax
import jax.numpy as jnp
from jax import lax
from jax.experimental import pallas as pl
from jax.experimental.pallas import tpu as pltpu
from jax.sharding import PartitionSpec as P

BLK = 128
MESH = pl.DeviceIdType.MESH
NZ, NX = 4, 2


def expand_blocks(table, rows, cols):
    row_blocks, col_blocks = table.shape
    spread = jnp.broadcast_to(table[:, None, :, None], (row_blocks, BLK, col_blocks, BLK))
    return spread.reshape(rows, cols)


def soft_weights(rounding, codes, scales, pick):
    rows, half = rounding.shape
    nblocks = half // BLK
    levels = (codes - 8).astype(jnp.float32)
    soft = jax.nn.sigmoid(rounding.astype(jnp.float32))
    factor = expand_blocks(scales, rows, half)
    kept_weight = (factor * jnp.clip(levels + soft, -8.0, 7.0)).astype(jnp.bfloat16)
    chosen = expand_blocks(pick, rows, half).reshape(rows, nblocks, 1, BLK)
    places = jnp.arange(2, dtype=jnp.int32).reshape(1, 1, 2, 1)
    spread = jnp.broadcast_to(kept_weight.reshape(rows, nblocks, 1, BLK), (rows, nblocks, 2, BLK))
    weight = jnp.where(chosen == places, spread, jnp.zeros((), jnp.bfloat16)).reshape(
        rows, 2 * half
    )
    slope = soft * (1.0 - soft) * (levels < 6.5).astype(jnp.float32)
    return (weight, slope, chosen)


def compact(full, chosen):
    rows = full.shape[0]
    nblocks = chosen.shape[1]
    pieces = full.reshape(rows, nblocks, 2, BLK)
    return jnp.where(chosen[:, :, 0, :] == 0, pieces[:, :, 0, :], pieces[:, :, 1, :]).reshape(
        rows, nblocks * BLK
    )


def body(inputs, rounding, codes, scales, pick, target):
    weight, slope, chosen = soft_weights(rounding, codes, scales, pick)
    tok_rows = inputs.shape[0]
    scale_root = math.sqrt(tok_rows * lax.axis_size("dp"))
    gathered = lax.all_gather(inputs, "mp", axis=1, tiled=True)
    columns = gathered
    outputs = jnp.dot(
        columns,
        lax.all_gather(weight, "dp", axis=0, tiled=True),
        preferred_element_type=jnp.float32,
    )
    resid = ((outputs - target.astype(jnp.float32)) / scale_root).astype(jnp.bfloat16)
    columns = gathered
    weight_grad = lax.psum_scatter(
        lax.dot_general(
            columns, resid, (((0,), (0,)), ((), ())), preferred_element_type=jnp.float32
        ).astype(jnp.bfloat16),
        "dp",
        scatter_dimension=0,
        tiled=True,
    ).astype(jnp.float32)
    return (compact(weight_grad, chosen) * slope).astype(jnp.bfloat16)


def order(step, z):
    far = z // 2
    near = z * (1 - far) + (NZ - 1 - z) * far
    late = step // 2
    place = (1 - late) * ((step + near) % 2) + late * step
    return (1 - far) * place + far * (NZ - 1 - place)


def kernel(
    inputs, rounding, codes, scales, pick, target, out,
    gathered, turned, weight, slope, rounding_v, codes_v, outputs, resid,
    pick_own, scale_rows, turned_other, resid_other, kept,
    local_sem, recv_sem, x_sem, up_sem, down_sem, w_send, w_recv, r_send, r_recv, t_send, t_recv,
):
    tokens, features = inputs.shape
    rows = rounding.shape[0]
    shards_each = rows // features
    blocks = features // BLK
    me = lax.axis_index("mp")
    dp = lax.axis_index("dp")
    z, x = me // NX, me % NX
    other = 1 - dp
    beside = {"mp": z * NX + (1 - x)}
    above = {"mp": me + NX}
    below = {"mp": me - NX}
    twin = {"dp": other}

    def remote(source, dest, send, recv, device):
        return pltpu.make_async_remote_copy(
            src_ref=source, dst_ref=dest, send_sem=send, recv_sem=recv,
            device_id=device, device_id_type=MESH,
        )

    own = pltpu.make_async_copy(inputs, gathered.at[me], local_sem.at[0])
    get_rounding = pltpu.make_async_copy(rounding, rounding_v, local_sem.at[1])
    get_codes = pltpu.make_async_copy(codes, codes_v, local_sem.at[2])
    own.start()
    get_rounding.start()
    get_codes.start()

    barrier = pltpu.get_barrier_semaphore()
    pl.semaphore_signal(barrier, inc=1, device_id=beside, device_id_type=MESH)
    pl.semaphore_signal(barrier, inc=1, device_id=twin, device_id_type=MESH)

    @pl.when(z < NZ - 1)
    def _():
        pl.semaphore_signal(barrier, inc=1, device_id=above, device_id_type=MESH)

    @pl.when(z > 0)
    def _():
        pl.semaphore_signal(barrier, inc=1, device_id=below, device_id_type=MESH)

    pl.semaphore_wait(barrier, 2 + (z + NZ - 2) // (NZ - 1) + (2 * NZ - 3 - z) // (NZ - 1))

    lead = tokens * 5 // 512 * 16
    middle = lead + (tokens - lead + 16) // 32 * 16
    bounds = ((lead, middle), (middle, tokens), (0, lead))

    def piece_copies(step, side, piece, fresh=False):
        column = order(step, z)
        slot = column * NX + (x if side == 0 else 1 - x)
        start, stop = bounds[piece]
        block = gathered.at[slot, pl.ds(start, stop - start), :]
        source = inputs.at[pl.ds(start, stop - start), :] if fresh else block
        arrive = recv_sem.at[slot, piece]
        lane = piece + side
        return (
            (column <= z, z < NZ - 1, lambda: remote(source, block, up_sem.at[step, lane], arrive, above)),
            (column >= z, z > 0, lambda: remote(source, block, down_sem.at[step, lane], arrive, below)),
            lambda: remote(source, block, x_sem.at[step, piece], arrive, beside),
        )

    def along(step, side, piece, act, fresh=False):
        for first, second, copy in piece_copies(step, side, piece, fresh)[:2]:

            @pl.when(jnp.logical_and(first, second))
            def _():
                act(copy())

    def across(step, piece, act, fresh=False):
        act(piece_copies(step, 0, piece, fresh)[2]())

    def arrived(step, side, piece):
        piece_copies(step, side, piece)[2]().wait_recv()

    def begin(copy):
        copy.start()

    across(0, 2, begin, True)
    for piece in range(3):
        along(0, 0, piece, begin, True)
        if piece < 2:
            across(0, piece, begin, True)

    across_lanes = (BLK, rows // BLK)
    pick_own[...] = jnp.broadcast_to(pick[...].astype(jnp.float32), across_lanes).T
    scale_rows[...] = jnp.broadcast_to(scales[...], across_lanes).T
    get_rounding.wait()
    get_codes.wait()

    def soft_block(index, carry):
        at = pl.ds(pl.multiple_of(index * BLK, BLK), BLK)
        levels = (codes_v[at, :] - 8).astype(jnp.float32)
        soft = jax.nn.sigmoid(rounding_v[at, :].astype(jnp.float32))
        factor = scale_rows[pl.ds(index, 1), :]
        chosen = pick_own[pl.ds(index, 1), :]
        value = factor * jnp.clip(levels + soft, -8.0, 7.0)
        first = jnp.broadcast_to(chosen, value.shape) < 0.5
        here = pl.ds(pl.multiple_of(dp * rows + index * BLK, BLK), BLK)
        weight[here, :BLK] = jnp.where(first, value, 0.0).astype(jnp.bfloat16)
        weight[here, BLK:] = jnp.where(first, 0.0, value).astype(jnp.bfloat16)
        slope[at, :] = soft * (1.0 - soft) * (levels < 6.5).astype(jnp.float32)
        return carry

    lax.fori_loop(0, rows // BLK, soft_block, 0)
    mine = weight.at[pl.ds(pl.multiple_of(dp * rows, BLK), rows), :]
    send_weight = remote(mine, mine, w_send, w_recv, twin)
    send_weight.start()
    arrived(0, 1, 2)
    along(0, 1, 2, begin)
    outputs[...] = jnp.zeros_like(outputs)
    send_weight.wait()

    width = 2 * BLK
    steps = features // width

    def turned_copy(slot):
        place = slot % shards_each
        return remote(
            turned.at[pl.ds(pl.multiple_of(slot * features, features), features), :],
            turned_other.at[pl.ds(pl.multiple_of(place * features, features), features), :],
            t_send.at[place], t_recv.at[place], twin,
        )

    def add(slot):
        def part(index, carry):
            at = pl.ds(pl.multiple_of(index * width, width), width)
            here = pl.ds(pl.multiple_of(slot * features + index * width, width), width)
            piece = gathered[slot, :, at]
            outputs[...] += jnp.dot(piece, weight[here, :], preferred_element_type=jnp.float32)
            turned[here, :] = piece.T
            return carry

        lax.fori_loop(0, steps, part, 0)

        @pl.when(slot // shards_each == other)
        def _():
            turned_copy(slot).start()

    own.wait()
    add(me)

    def column_step(step, carry):
        for piece in range(2):
            arrived(step, 0, piece)
            along(step, 0, piece, begin)
            across(step, piece, begin)
        return carry

    lax.fori_loop(1, NZ, column_step, 0)
    for piece in range(2):
        arrived(0, 1, piece)
    add(z * NX + 1 - x)

    def lead_step(step, carry):
        for side in range(2):
            arrived(step, side, 2)
            along(step, side, 2, begin)
        column = order(step, z)
        add(column * NX + x)
        for piece in range(2):
            arrived(step, 1, piece)
        add(column * NX + 1 - x)
        return carry

    lax.fori_loop(1, NZ, lead_step, 0)

    scale_root = math.sqrt(tokens * 2)
    resid[...] = ((outputs[...] - target[...].astype(jnp.float32)) / scale_root).astype(jnp.bfloat16)

    send_resid = remote(resid, resid_other, r_send, r_recv, twin)
    send_resid.start()

    def block_grad(rows_of, start, index, errors):
        here = pl.ds(pl.multiple_of(start + index * width, width), width)
        full = jnp.dot(rows_of[here, :], errors[...], preferred_element_type=jnp.float32)
        parts = []
        for half in range(2):
            chosen = pick_own[pl.ds(2 * index + half, 1), :]
            piece = full[half * BLK:(half + 1) * BLK]
            first = jnp.broadcast_to(chosen, (BLK, BLK)) < 0.5
            parts.append(jnp.where(first, piece[:, :BLK], piece[:, BLK:]).astype(jnp.bfloat16))
        return parts

    def keep(index, carry):
        for half, term in enumerate(block_grad(turned, dp * rows, index, resid)):
            kept[pl.ds(pl.multiple_of(index * width + half * BLK, BLK), BLK), :] = term
        return carry

    lax.fori_loop(0, shards_each * steps, keep, 0)
    send_resid.wait()

    def finish(turn, carry):
        far = z // 2
        place = (1 - far) * turn + far * (shards_each - 1 - turn)
        turned_copy(dp * shards_each + place).wait_recv()

        def part(index, carry):
            index = place * steps + index
            for half, term in enumerate(block_grad(turned_other, 0, index, resid_other)):
                at = pl.ds(pl.multiple_of(index * width + half * BLK, BLK), BLK)
                total = kept[at, :].astype(jnp.float32) + term.astype(jnp.float32)
                out[at, :] = (total * slope[at, :]).astype(jnp.bfloat16)
            return carry

        return lax.fori_loop(0, steps, part, carry)

    lax.fori_loop(0, shards_each, finish, 0)

    def sent(place, carry):
        turned_copy(other * shards_each + place).wait_send()
        return carry

    lax.fori_loop(0, shards_each, sent, 0)

    def finished(copy):
        copy.wait_send()

    def drain(step, carry):
        for piece in range(3):
            along(step, 0, piece, finished)
        along(step, 1, 2, finished)
        for piece in range(2):
            across(step, piece, finished)
        return carry

    across(0, 2, finished)
    lax.fori_loop(0, NZ, drain, 0)


def fused(inputs, rounding, codes, scales, pick, target):
    tokens, features = inputs.shape
    rows = rounding.shape[0]
    shards = NZ * NX
    every = shards * features
    anywhere = pl.BlockSpec(memory_space=pltpu.HBM)
    near = pl.BlockSpec(memory_space=pltpu.VMEM)
    bf16, f32 = jnp.bfloat16, jnp.float32
    dma = pltpu.SemaphoreType.DMA
    return pl.pallas_call(
        kernel,
        out_shape=jax.ShapeDtypeStruct((rows, BLK), bf16),
        in_specs=[anywhere, anywhere, anywhere, near, near, near],
        out_specs=near,
        scratch_shapes=[
            pltpu.VMEM((shards, tokens, features), bf16),
            pltpu.VMEM((every, tokens), bf16),
            pltpu.VMEM((every, 2 * BLK), bf16),
            pltpu.VMEM((rows, BLK), f32),
            pltpu.VMEM((rows, BLK), bf16),
            pltpu.VMEM((rows, BLK), jnp.int32),
            pltpu.VMEM((tokens, 2 * BLK), f32),
            pltpu.VMEM((tokens, 2 * BLK), bf16),
            pltpu.VMEM((rows // BLK, BLK), f32),
            pltpu.VMEM((rows // BLK, BLK), f32),
            pltpu.VMEM((rows, tokens), bf16),
            pltpu.VMEM((tokens, 2 * BLK), bf16),
            pltpu.VMEM((rows, BLK), bf16),
            dma((3,)),
            dma((shards, 3)),
            dma((NZ, 3)),
            dma((NZ, 4)),
            dma((NZ, 4)),
            dma(()),
            dma(()),
            dma(()),
            dma(()),
            dma((rows // features,)),
            dma((rows // features,)),
        ],
        compiler_params=pltpu.CompilerParams(
            collective_id=0, has_side_effects=True, vmem_limit_bytes=60 * 1024 * 1024
        ),
    )(inputs, rounding, codes, scales.T, pick.T, target)


def solution(mesh):
    grid = mesh.shape["mp"] == NZ * NX and mesh.shape["dp"] == 2
    run = fused if grid else body
    in_specs = (
        P(("groups", "dp"), "mp"),
        P(("groups", "dp"), "mp"),
        P(("groups", "dp"), "mp"),
        P(("groups", "dp"), "mp"),
        P(("groups", "dp"), "mp"),
        P(("groups", "dp"), "mp"),
    )
    out_specs = P(("groups", "dp"), "mp")
    return jax.shard_map(run, mesh=mesh, in_specs=in_specs, out_specs=out_specs, check_vma=False)
```

```python
import math

import jax
import jax.numpy as jnp
from jax import lax
from jax.experimental import pallas as pl
from jax.experimental.pallas import tpu as pltpu
from jax.sharding import PartitionSpec as P

BLK = 128
MESH = pl.DeviceIdType.MESH
NZ, NX = 4, 2


def expand_blocks(table, rows, cols):
    row_blocks, col_blocks = table.shape
    spread = jnp.broadcast_to(table[:, None, :, None], (row_blocks, BLK, col_blocks, BLK))
    return spread.reshape(rows, cols)


def soft_weights(rounding, codes, scales, pick):
    rows, half = rounding.shape
    nblocks = half // BLK
    levels = (codes - 8).astype(jnp.float32)
    soft = jax.nn.sigmoid(rounding.astype(jnp.float32))
    factor = expand_blocks(scales, rows, half)
    kept_weight = (factor * jnp.clip(levels + soft, -8.0, 7.0)).astype(jnp.bfloat16)
    chosen = expand_blocks(pick, rows, half).reshape(rows, nblocks, 1, BLK)
    places = jnp.arange(2, dtype=jnp.int32).reshape(1, 1, 2, 1)
    spread = jnp.broadcast_to(kept_weight.reshape(rows, nblocks, 1, BLK), (rows, nblocks, 2, BLK))
    weight = jnp.where(chosen == places, spread, jnp.zeros((), jnp.bfloat16)).reshape(
        rows, 2 * half
    )
    slope = soft * (1.0 - soft) * (levels < 6.5).astype(jnp.float32)
    return (weight, slope, chosen)


def compact(full, chosen):
    rows = full.shape[0]
    nblocks = chosen.shape[1]
    pieces = full.reshape(rows, nblocks, 2, BLK)
    return jnp.where(chosen[:, :, 0, :] == 0, pieces[:, :, 0, :], pieces[:, :, 1, :]).reshape(
        rows, nblocks * BLK
    )


def body(inputs, rounding, codes, scales, pick, target):
    weight, slope, chosen = soft_weights(rounding, codes, scales, pick)
    tok_rows = inputs.shape[0]
    scale_root = math.sqrt(tok_rows * lax.axis_size("dp"))
    gathered = lax.all_gather(inputs, "mp", axis=1, tiled=True)
    columns = gathered
    outputs = jnp.dot(
        columns,
        lax.all_gather(weight, "dp", axis=0, tiled=True),
        preferred_element_type=jnp.float32,
    )
    resid = ((outputs - target.astype(jnp.float32)) / scale_root).astype(jnp.bfloat16)
    columns = gathered
    weight_grad = lax.psum_scatter(
        lax.dot_general(
            columns, resid, (((0,), (0,)), ((), ())), preferred_element_type=jnp.float32
        ).astype(jnp.bfloat16),
        "dp",
        scatter_dimension=0,
        tiled=True,
    ).astype(jnp.float32)
    return (compact(weight_grad, chosen) * slope).astype(jnp.bfloat16)


def order(step, z):
    far = z // 2
    near = z * (1 - far) + (NZ - 1 - z) * far
    late = step // 2
    place = (1 - late) * ((step + near) % 2) + late * step
    return (1 - far) * place + far * (NZ - 1 - place)


def kernel(
    inputs, rounding, codes, scales, pick, target, out,
    gathered, turned, weight, slope, rounding_v, codes_v, outputs, resid,
    pick_own, scale_rows, turned_other, resid_other, kept, result,
    local_sem, recv_sem, x_sem, up_sem, down_sem, w_send, w_recv, r_send, r_recv, t_send, t_recv, out_sem,
):
    tokens, features = inputs.shape
    rows = rounding.shape[0]
    shards_each = rows // features
    blocks = features // BLK
    me = lax.axis_index("mp")
    dp = lax.axis_index("dp")
    z, x = me // NX, me % NX
    other = 1 - dp
    beside = {"mp": z * NX + (1 - x)}
    above = {"mp": me + NX}
    below = {"mp": me - NX}
    twin = {"dp": other}

    def remote(source, dest, send, recv, device):
        return pltpu.make_async_remote_copy(
            src_ref=source, dst_ref=dest, send_sem=send, recv_sem=recv,
            device_id=device, device_id_type=MESH,
        )

    own = pltpu.make_async_copy(inputs, gathered.at[me], local_sem.at[0])
    get_rounding = pltpu.make_async_copy(rounding, rounding_v, local_sem.at[1])
    get_codes = pltpu.make_async_copy(codes, codes_v, local_sem.at[2])
    own.start()
    get_rounding.start()
    get_codes.start()

    barrier = pltpu.get_barrier_semaphore()
    pl.semaphore_signal(barrier, inc=1, device_id=beside, device_id_type=MESH)
    pl.semaphore_signal(barrier, inc=1, device_id=twin, device_id_type=MESH)

    @pl.when(z < NZ - 1)
    def _():
        pl.semaphore_signal(barrier, inc=1, device_id=above, device_id_type=MESH)

    @pl.when(z > 0)
    def _():
        pl.semaphore_signal(barrier, inc=1, device_id=below, device_id_type=MESH)

    pl.semaphore_wait(barrier, 2 + (z + NZ - 2) // (NZ - 1) + (2 * NZ - 3 - z) // (NZ - 1))

    lead = tokens * 5 // 512 * 16
    middle = lead + (tokens - lead + 16) // 32 * 16
    bounds = ((lead, middle), (middle, tokens), (0, lead))

    def piece_copies(step, side, piece, fresh=False):
        column = order(step, z)
        slot = column * NX + (x if side == 0 else 1 - x)
        start, stop = bounds[piece]
        block = gathered.at[slot, pl.ds(start, stop - start), :]
        source = inputs.at[pl.ds(start, stop - start), :] if fresh else block
        arrive = recv_sem.at[slot, piece]
        lane = piece + side
        return (
            (column <= z, z < NZ - 1, lambda: remote(source, block, up_sem.at[step, lane], arrive, above)),
            (column >= z, z > 0, lambda: remote(source, block, down_sem.at[step, lane], arrive, below)),
            lambda: remote(source, block, x_sem.at[step, piece], arrive, beside),
        )

    def along(step, side, piece, act, fresh=False):
        for first, second, copy in piece_copies(step, side, piece, fresh)[:2]:

            @pl.when(jnp.logical_and(first, second))
            def _():
                act(copy())

    def across(step, piece, act, fresh=False):
        act(piece_copies(step, 0, piece, fresh)[2]())

    def arrived(step, side, piece):
        piece_copies(step, side, piece)[2]().wait_recv()

    def begin(copy):
        copy.start()

    across(0, 2, begin, True)
    for piece in range(3):
        along(0, 0, piece, begin, True)
        if piece < 2:
            across(0, piece, begin, True)

    across_lanes = (BLK, rows // BLK)
    pick_own[...] = jnp.broadcast_to(pick[...].astype(jnp.float32), across_lanes).T
    scale_rows[...] = jnp.broadcast_to(scales[...], across_lanes).T
    get_rounding.wait()
    get_codes.wait()

    def soft_block(index, carry):
        at = pl.ds(pl.multiple_of(index * BLK, BLK), BLK)
        levels = (codes_v[at, :] - 8).astype(jnp.float32)
        soft = jax.nn.sigmoid(rounding_v[at, :].astype(jnp.float32))
        factor = scale_rows[pl.ds(index, 1), :]
        chosen = pick_own[pl.ds(index, 1), :]
        value = factor * jnp.clip(levels + soft, -8.0, 7.0)
        first = jnp.broadcast_to(chosen, value.shape) < 0.5
        here = pl.ds(pl.multiple_of(dp * rows + index * BLK, BLK), BLK)
        weight[here, :BLK] = jnp.where(first, value, 0.0).astype(jnp.bfloat16)
        weight[here, BLK:] = jnp.where(first, 0.0, value).astype(jnp.bfloat16)
        slope[at, :] = soft * (1.0 - soft) * (levels < 6.5).astype(jnp.float32)
        return carry

    lax.fori_loop(0, rows // BLK, soft_block, 0)
    mine = weight.at[pl.ds(pl.multiple_of(dp * rows, BLK), rows), :]
    send_weight = remote(mine, mine, w_send, w_recv, twin)
    send_weight.start()
    arrived(0, 1, 2)
    along(0, 1, 2, begin)
    outputs[...] = jnp.zeros_like(outputs)
    send_weight.wait()

    width = 2 * BLK
    steps = features // width

    def turned_copy(slot):
        place = slot % shards_each
        return remote(
            turned.at[pl.ds(pl.multiple_of(slot * features, features), features), :],
            turned_other.at[pl.ds(pl.multiple_of(place * features, features), features), :],
            t_send.at[place], t_recv.at[place], twin,
        )

    def add(slot):
        def part(index, carry):
            at = pl.ds(pl.multiple_of(index * width, width), width)
            here = pl.ds(pl.multiple_of(slot * features + index * width, width), width)
            piece = gathered[slot, :, at]
            outputs[...] += jnp.dot(piece, weight[here, :], preferred_element_type=jnp.float32)
            turned[here, :] = piece.T
            return carry

        lax.fori_loop(0, steps, part, 0, unroll=4)

        @pl.when(slot // shards_each == other)
        def _():
            turned_copy(slot).start()

    own.wait()
    add(me)

    def column_step(step, carry):
        for piece in range(2):
            arrived(step, 0, piece)
            along(step, 0, piece, begin)
            across(step, piece, begin)
        return carry

    lax.fori_loop(1, NZ, column_step, 0)
    for piece in range(2):
        arrived(0, 1, piece)
    add(z * NX + 1 - x)

    def lead_step(step, carry):
        for side in range(2):
            arrived(step, side, 2)
            along(step, side, 2, begin)
        column = order(step, z)
        add(column * NX + x)
        for piece in range(2):
            arrived(step, 1, piece)
        add(column * NX + 1 - x)
        return carry

    lax.fori_loop(1, NZ, lead_step, 0)

    scale_root = math.sqrt(tokens * 2)
    resid[...] = ((outputs[...] - target[...].astype(jnp.float32)) / scale_root).astype(jnp.bfloat16)

    send_resid = remote(resid, resid_other, r_send, r_recv, twin)
    send_resid.start()

    def block_grad(rows_of, start, index, errors):
        here = pl.ds(pl.multiple_of(start + index * width, width), width)
        full = jnp.dot(rows_of[here, :], errors[...], preferred_element_type=jnp.float32)
        parts = []
        for half in range(2):
            chosen = pick_own[pl.ds(2 * index + half, 1), :]
            piece = full[half * BLK:(half + 1) * BLK]
            first = jnp.broadcast_to(chosen, (BLK, BLK)) < 0.5
            parts.append(jnp.where(first, piece[:, :BLK], piece[:, BLK:]).astype(jnp.bfloat16))
        return parts

    def keep(index, carry):
        for half, term in enumerate(block_grad(turned, dp * rows, index, resid)):
            kept[pl.ds(pl.multiple_of(index * width + half * BLK, BLK), BLK), :] = term
        return carry

    lax.fori_loop(0, shards_each * steps, keep, 0, unroll=4)
    send_resid.wait()

    def finish(turn, carry):
        far = z // 2
        place = (1 - far) * turn + far * (shards_each - 1 - turn)
        turned_copy(dp * shards_each + place).wait_recv()

        def part(index, carry):
            index = place * steps + index
            for half, term in enumerate(block_grad(turned_other, 0, index, resid_other)):
                at = pl.ds(pl.multiple_of(index * width + half * BLK, BLK), BLK)
                total = kept[at, :].astype(jnp.float32) + term.astype(jnp.float32)
                result[at, :] = (total * slope[at, :]).astype(jnp.bfloat16)
            return carry

        lax.fori_loop(0, steps, part, 0, unroll=4)
        put(place).start()
        return carry

    def put(place):
        at = pl.ds(pl.multiple_of(place * features, features), features)
        return pltpu.make_async_copy(result.at[at, :], out.at[at, :], out_sem.at[place])

    lax.fori_loop(0, shards_each, finish, 0)

    def sent(place, carry):
        turned_copy(other * shards_each + place).wait_send()
        put(place).wait()
        return carry

    lax.fori_loop(0, shards_each, sent, 0)

    def finished(copy):
        copy.wait_send()

    def drain(step, carry):
        for piece in range(3):
            along(step, 0, piece, finished)
        along(step, 1, 2, finished)
        for piece in range(2):
            across(step, piece, finished)
        return carry

    across(0, 2, finished)
    lax.fori_loop(0, NZ, drain, 0)


def fused(inputs, rounding, codes, scales, pick, target):
    tokens, features = inputs.shape
    rows = rounding.shape[0]
    shards = NZ * NX
    every = shards * features
    anywhere = pl.BlockSpec(memory_space=pltpu.HBM)
    near = pl.BlockSpec(memory_space=pltpu.VMEM)
    bf16, f32 = jnp.bfloat16, jnp.float32
    dma = pltpu.SemaphoreType.DMA
    return pl.pallas_call(
        kernel,
        out_shape=jax.ShapeDtypeStruct((rows, BLK), bf16),
        in_specs=[anywhere, anywhere, anywhere, near, near, near],
        out_specs=anywhere,
        scratch_shapes=[
            pltpu.VMEM((shards, tokens, features), bf16),
            pltpu.VMEM((every, tokens), bf16),
            pltpu.VMEM((every, 2 * BLK), bf16),
            pltpu.VMEM((rows, BLK), f32),
            pltpu.VMEM((rows, BLK), bf16),
            pltpu.VMEM((rows, BLK), jnp.int32),
            pltpu.VMEM((tokens, 2 * BLK), f32),
            pltpu.VMEM((tokens, 2 * BLK), bf16),
            pltpu.VMEM((rows // BLK, BLK), f32),
            pltpu.VMEM((rows // BLK, BLK), f32),
            pltpu.VMEM((rows, tokens), bf16),
            pltpu.VMEM((tokens, 2 * BLK), bf16),
            pltpu.VMEM((rows, BLK), bf16),
            pltpu.VMEM((rows, BLK), bf16),
            dma((3,)),
            dma((shards, 3)),
            dma((NZ, 3)),
            dma((NZ, 4)),
            dma((NZ, 4)),
            dma(()),
            dma(()),
            dma(()),
            dma(()),
            dma((rows // features,)),
            dma((rows // features,)),
            dma((rows // features,)),
        ],
        compiler_params=pltpu.CompilerParams(
            collective_id=0, has_side_effects=True, vmem_limit_bytes=60 * 1024 * 1024
        ),
    )(inputs, rounding, codes, scales.T, pick.T, target)


def solution(mesh):
    grid = mesh.shape["mp"] == NZ * NX and mesh.shape["dp"] == 2
    run = fused if grid else body
    in_specs = (
        P(("groups", "dp"), "mp"),
        P(("groups", "dp"), "mp"),
        P(("groups", "dp"), "mp"),
        P(("groups", "dp"), "mp"),
        P(("groups", "dp"), "mp"),
        P(("groups", "dp"), "mp"),
    )
    out_specs = P(("groups", "dp"), "mp")
    return jax.shard_map(run, mesh=mesh, in_specs=in_specs, out_specs=out_specs, check_vma=False)
```

```python
import math

import jax
import jax.numpy as jnp
from jax import lax
from jax.experimental import pallas as pl
from jax.experimental.pallas import tpu as pltpu
from jax.sharding import PartitionSpec as P

BLK = 128
MESH = pl.DeviceIdType.MESH
NZ, NX = 4, 2


def expand_blocks(table, rows, cols):
    row_blocks, col_blocks = table.shape
    spread = jnp.broadcast_to(table[:, None, :, None], (row_blocks, BLK, col_blocks, BLK))
    return spread.reshape(rows, cols)


def soft_weights(rounding, codes, scales, pick):
    rows, half = rounding.shape
    nblocks = half // BLK
    levels = (codes - 8).astype(jnp.float32)
    soft = jax.nn.sigmoid(rounding.astype(jnp.float32))
    factor = expand_blocks(scales, rows, half)
    kept_weight = (factor * jnp.clip(levels + soft, -8.0, 7.0)).astype(jnp.bfloat16)
    chosen = expand_blocks(pick, rows, half).reshape(rows, nblocks, 1, BLK)
    places = jnp.arange(2, dtype=jnp.int32).reshape(1, 1, 2, 1)
    spread = jnp.broadcast_to(kept_weight.reshape(rows, nblocks, 1, BLK), (rows, nblocks, 2, BLK))
    weight = jnp.where(chosen == places, spread, jnp.zeros((), jnp.bfloat16)).reshape(
        rows, 2 * half
    )
    slope = soft * (1.0 - soft) * (levels < 6.5).astype(jnp.float32)
    return (weight, slope, chosen)


def compact(full, chosen):
    rows = full.shape[0]
    nblocks = chosen.shape[1]
    pieces = full.reshape(rows, nblocks, 2, BLK)
    return jnp.where(chosen[:, :, 0, :] == 0, pieces[:, :, 0, :], pieces[:, :, 1, :]).reshape(
        rows, nblocks * BLK
    )


def body(inputs, rounding, codes, scales, pick, target):
    weight, slope, chosen = soft_weights(rounding, codes, scales, pick)
    tok_rows = inputs.shape[0]
    scale_root = math.sqrt(tok_rows * lax.axis_size("dp"))
    gathered = lax.all_gather(inputs, "mp", axis=1, tiled=True)
    columns = gathered
    outputs = jnp.dot(
        columns,
        lax.all_gather(weight, "dp", axis=0, tiled=True),
        preferred_element_type=jnp.float32,
    )
    resid = ((outputs - target.astype(jnp.float32)) / scale_root).astype(jnp.bfloat16)
    columns = gathered
    weight_grad = lax.psum_scatter(
        lax.dot_general(
            columns, resid, (((0,), (0,)), ((), ())), preferred_element_type=jnp.float32
        ).astype(jnp.bfloat16),
        "dp",
        scatter_dimension=0,
        tiled=True,
    ).astype(jnp.float32)
    return (compact(weight_grad, chosen) * slope).astype(jnp.bfloat16)


def order(step, z):
    far = z // 2
    near = z * (1 - far) + (NZ - 1 - z) * far
    late = step // 2
    place = (1 - late) * ((step + near) % 2) + late * step
    return (1 - far) * place + far * (NZ - 1 - place)


def kernel(
    inputs, rounding, codes, scales, pick, target, out,
    gathered, turned, weight, slope, rounding_v, codes_v, outputs, resid,
    pick_own, scale_rows, turned_other, resid_other, kept, result,
    local_sem, recv_sem, x_sem, up_sem, down_sem, w_send, w_recv, r_send, r_recv, t_send, t_recv, out_sem,
):
    tokens, features = inputs.shape
    rows = rounding.shape[0]
    shards_each = rows // features
    blocks = features // BLK
    me = lax.axis_index("mp")
    dp = lax.axis_index("dp")
    z, x = me // NX, me % NX
    other = 1 - dp
    beside = {"mp": z * NX + (1 - x)}
    above = {"mp": me + NX}
    below = {"mp": me - NX}
    twin = {"dp": other}

    def remote(source, dest, send, recv, device):
        return pltpu.make_async_remote_copy(
            src_ref=source, dst_ref=dest, send_sem=send, recv_sem=recv,
            device_id=device, device_id_type=MESH,
        )

    own = pltpu.make_async_copy(inputs, gathered.at[me], local_sem.at[0])
    get_rounding = pltpu.make_async_copy(rounding, rounding_v, local_sem.at[1])
    get_codes = pltpu.make_async_copy(codes, codes_v, local_sem.at[2])
    own.start()
    get_rounding.start()
    get_codes.start()

    barrier = pltpu.get_barrier_semaphore()
    pl.semaphore_signal(barrier, inc=1, device_id=beside, device_id_type=MESH)
    pl.semaphore_signal(barrier, inc=1, device_id=twin, device_id_type=MESH)

    @pl.when(z < NZ - 1)
    def _():
        pl.semaphore_signal(barrier, inc=1, device_id=above, device_id_type=MESH)

    @pl.when(z > 0)
    def _():
        pl.semaphore_signal(barrier, inc=1, device_id=below, device_id_type=MESH)

    pl.semaphore_wait(barrier, 2 + (z + NZ - 2) // (NZ - 1) + (2 * NZ - 3 - z) // (NZ - 1))

    lead = tokens * 5 // 512 * 16
    middle = tokens // 2
    bounds = ((lead, middle), (middle, tokens), (0, lead))

    def piece_copies(step, side, piece, fresh=False):
        column = order(step, z)
        slot = column * NX + (x if side == 0 else 1 - x)
        start, stop = bounds[piece]
        block = gathered.at[slot, pl.ds(start, stop - start), :]
        source = inputs.at[pl.ds(start, stop - start), :] if fresh else block
        arrive = recv_sem.at[slot, piece]
        lane = piece + side
        return (
            (column <= z, z < NZ - 1, lambda: remote(source, block, up_sem.at[step, lane], arrive, above)),
            (column >= z, z > 0, lambda: remote(source, block, down_sem.at[step, lane], arrive, below)),
            lambda: remote(source, block, x_sem.at[step, piece], arrive, beside),
        )

    def along(step, side, piece, act, fresh=False):
        for first, second, copy in piece_copies(step, side, piece, fresh)[:2]:

            @pl.when(jnp.logical_and(first, second))
            def _():
                act(copy())

    def across(step, piece, act, fresh=False):
        act(piece_copies(step, 0, piece, fresh)[2]())

    def arrived(step, side, piece):
        piece_copies(step, side, piece)[2]().wait_recv()

    def begin(copy):
        copy.start()

    across(0, 2, begin, True)
    for piece in range(3):
        along(0, 0, piece, begin, True)
        if piece < 2:
            across(0, piece, begin, True)

    across_lanes = (BLK, rows // BLK)
    pick_own[...] = jnp.broadcast_to(pick[...].astype(jnp.float32), across_lanes).T
    scale_rows[...] = jnp.broadcast_to(scales[...], across_lanes).T
    get_rounding.wait()
    get_codes.wait()

    def soft_block(index, carry):
        at = pl.ds(pl.multiple_of(index * BLK, BLK), BLK)
        levels = (codes_v[at, :] - 8).astype(jnp.float32)
        soft = jax.nn.sigmoid(rounding_v[at, :].astype(jnp.float32))
        factor = scale_rows[pl.ds(index, 1), :]
        chosen = pick_own[pl.ds(index, 1), :]
        value = factor * jnp.clip(levels + soft, -8.0, 7.0)
        first = jnp.broadcast_to(chosen, value.shape) < 0.5
        here = pl.ds(pl.multiple_of(dp * rows + index * BLK, BLK), BLK)
        weight[here, :BLK] = jnp.where(first, value, 0.0).astype(jnp.bfloat16)
        weight[here, BLK:] = jnp.where(first, 0.0, value).astype(jnp.bfloat16)
        slope[at, :] = soft * (1.0 - soft) * (levels < 6.5).astype(jnp.float32)
        return carry

    lax.fori_loop(0, rows // BLK, soft_block, 0)
    mine = weight.at[pl.ds(pl.multiple_of(dp * rows, BLK), rows), :]
    send_weight = remote(mine, mine, w_send, w_recv, twin)
    send_weight.start()
    arrived(0, 1, 2)
    along(0, 1, 2, begin)
    outputs[...] = jnp.zeros_like(outputs)
    send_weight.wait()

    width = 2 * BLK
    steps = features // width

    def turned_copy(slot, half):
        place = slot % shards_each
        side = pl.ds(half * middle, middle)
        return remote(
            turned.at[pl.ds(pl.multiple_of(slot * features, features), features), side],
            turned_other.at[pl.ds(pl.multiple_of(place * features, features), features), side],
            t_send.at[place, half], t_recv.at[place, half], twin,
        )

    def add_half(slot, half):
        some = pl.ds(half * middle, middle)

        def part(index, carry):
            at = pl.ds(pl.multiple_of(index * width, width), width)
            here = pl.ds(pl.multiple_of(slot * features + index * width, width), width)
            piece = gathered[slot, some, at]
            outputs[some, :] += jnp.dot(piece, weight[here, :], preferred_element_type=jnp.float32)
            turned[here, some] = piece.T
            return carry

        lax.fori_loop(0, steps, part, 0, unroll=4)

        @pl.when(slot // shards_each == other)
        def _():
            turned_copy(slot, half).start()

    def add(slot):
        add_half(slot, 0)
        add_half(slot, 1)

    own.wait()
    add(me)

    def column_step(step, carry):
        for piece in range(2):
            arrived(step, 0, piece)
            along(step, 0, piece, begin)
            across(step, piece, begin)
        return carry

    lax.fori_loop(1, NZ, column_step, 0)
    for piece in range(2):
        arrived(0, 1, piece)
    add(z * NX + 1 - x)

    def lead_step(step, carry):
        for side in range(2):
            arrived(step, side, 2)
            along(step, side, 2, begin)
        column = order(step, z)
        add(column * NX + x)
        for piece in range(2):
            arrived(step, 1, piece)
            add_half(column * NX + 1 - x, piece)
        return carry

    lax.fori_loop(1, NZ, lead_step, 0)

    scale_root = math.sqrt(tokens * 2)
    resid[...] = ((outputs[...] - target[...].astype(jnp.float32)) / scale_root).astype(jnp.bfloat16)

    send_resid = remote(resid, resid_other, r_send, r_recv, twin)
    send_resid.start()

    def block_grad(rows_of, start, index, errors):
        here = pl.ds(pl.multiple_of(start + index * width, width), width)
        full = jnp.dot(rows_of[here, :], errors[...], preferred_element_type=jnp.float32)
        parts = []
        for half in range(2):
            chosen = pick_own[pl.ds(2 * index + half, 1), :]
            piece = full[half * BLK:(half + 1) * BLK]
            first = jnp.broadcast_to(chosen, (BLK, BLK)) < 0.5
            parts.append(jnp.where(first, piece[:, :BLK], piece[:, BLK:]).astype(jnp.bfloat16))
        return parts

    def keep(index, carry):
        for half, term in enumerate(block_grad(turned, dp * rows, index, resid)):
            kept[pl.ds(pl.multiple_of(index * width + half * BLK, BLK), BLK), :] = term
        return carry

    lax.fori_loop(0, shards_each * steps, keep, 0, unroll=4)
    send_resid.wait()

    def finish(turn, carry):
        far = z // 2
        place = (1 - far) * turn + far * (shards_each - 1 - turn)
        for half in range(2):
            turned_copy(dp * shards_each + place, half).wait_recv()

        def part(index, carry):
            index = place * steps + index
            for half, term in enumerate(block_grad(turned_other, 0, index, resid_other)):
                at = pl.ds(pl.multiple_of(index * width + half * BLK, BLK), BLK)
                total = kept[at, :].astype(jnp.float32) + term.astype(jnp.float32)
                result[at, :] = (total * slope[at, :]).astype(jnp.bfloat16)
            return carry

        lax.fori_loop(0, steps, part, 0, unroll=4)
        put(place).start()
        return carry

    def put(place):
        at = pl.ds(pl.multiple_of(place * features, features), features)
        return pltpu.make_async_copy(result.at[at, :], out.at[at, :], out_sem.at[place])

    lax.fori_loop(0, shards_each, finish, 0)

    def sent(place, carry):
        for half in range(2):
            turned_copy(other * shards_each + place, half).wait_send()
        put(place).wait()
        return carry

    lax.fori_loop(0, shards_each, sent, 0)

    def finished(copy):
        copy.wait_send()

    def drain(step, carry):
        for piece in range(3):
            along(step, 0, piece, finished)
        along(step, 1, 2, finished)
        for piece in range(2):
            across(step, piece, finished)
        return carry

    across(0, 2, finished)
    lax.fori_loop(0, NZ, drain, 0)


def fused(inputs, rounding, codes, scales, pick, target):
    tokens, features = inputs.shape
    rows = rounding.shape[0]
    shards = NZ * NX
    every = shards * features
    anywhere = pl.BlockSpec(memory_space=pltpu.HBM)
    near = pl.BlockSpec(memory_space=pltpu.VMEM)
    bf16, f32 = jnp.bfloat16, jnp.float32
    dma = pltpu.SemaphoreType.DMA
    return pl.pallas_call(
        kernel,
        out_shape=jax.ShapeDtypeStruct((rows, BLK), bf16),
        in_specs=[anywhere, anywhere, anywhere, near, near, near],
        out_specs=anywhere,
        scratch_shapes=[
            pltpu.VMEM((shards, tokens, features), bf16),
            pltpu.VMEM((every, tokens), bf16),
            pltpu.VMEM((every, 2 * BLK), bf16),
            pltpu.VMEM((rows, BLK), f32),
            pltpu.VMEM((rows, BLK), bf16),
            pltpu.VMEM((rows, BLK), jnp.int32),
            pltpu.VMEM((tokens, 2 * BLK), f32),
            pltpu.VMEM((tokens, 2 * BLK), bf16),
            pltpu.VMEM((rows // BLK, BLK), f32),
            pltpu.VMEM((rows // BLK, BLK), f32),
            pltpu.VMEM((rows, tokens), bf16),
            pltpu.VMEM((tokens, 2 * BLK), bf16),
            pltpu.VMEM((rows, BLK), bf16),
            pltpu.VMEM((rows, BLK), bf16),
            dma((3,)),
            dma((shards, 3)),
            dma((NZ, 3)),
            dma((NZ, 4)),
            dma((NZ, 4)),
            dma(()),
            dma(()),
            dma(()),
            dma(()),
            dma((rows // features, 2)),
            dma((rows // features, 2)),
            dma((rows // features,)),
        ],
        compiler_params=pltpu.CompilerParams(
            collective_id=0, has_side_effects=True, vmem_limit_bytes=60 * 1024 * 1024
        ),
    )(inputs, rounding, codes, scales.T, pick.T, target)


def solution(mesh):
    grid = mesh.shape["mp"] == NZ * NX and mesh.shape["dp"] == 2
    run = fused if grid else body
    in_specs = (
        P(("groups", "dp"), "mp"),
        P(("groups", "dp"), "mp"),
        P(("groups", "dp"), "mp"),
        P(("groups", "dp"), "mp"),
        P(("groups", "dp"), "mp"),
        P(("groups", "dp"), "mp"),
    )
    out_specs = P(("groups", "dp"), "mp")
    return jax.shard_map(run, mesh=mesh, in_specs=in_specs, out_specs=out_specs, check_vma=False)
```
